32 devices in a mesh: lat: 8 (over z, y), lon: 4 (over x, core).
Axes of the slice: x: 2, y: 2, z: 4, core: 2. Of those that a mesh axis runs over, the one named last changes fastest.
Arguments:
- prognostic: float32 [6, 2, 2304, 1024], P(None, None, 'lon', 'lat'), may hold values from -6 to 6
- wind_zonal: float32 [2, 1024], P(None, 'lat'), may hold values from -1 to 1
- wind_merid: float32 [2, 1024], P(None, 'lat'), may hold values from -0.5 to 0.5
- layer_depth: float32 [2], replicated, may hold values from 0.25 to 1
- diffusion: float32 [3, 2], replicated, may hold values from 0.05 to 0.4
Outputs:
- prognostic_out: float32 [6, 2, 2304, 1024], P(None, None, 'lon', 'lat')
The draws below stay inside these ranges and needn't reach their ends.
All inputs are finite; a program needn't handle non-finite values.
Results may differ from the reference program's by a relative error of at most 0.00013.
Values sent between devices are 32-bit elements; how exact they have to be, the bound alone decides.
A program may use at most 128 MiB of HBM per device.

```python
import math
import jax
import jax.numpy as jnp

NLON = 2304
FIELDS = 6
LEV = 2
ITERS = 3
NLAT = 1024


def levels(key, dims, split, smallest, largest):
    gain, own = 1.0, jax.random.fold_in(key, 6)
    for axis_at, shards_of in split:
        heights = jnp.exp(jax.random.uniform(jax.random.fold_in(own, axis_at), (shards_of,), jnp.float32, smallest / len(split), largest / len(split)))
        gain = gain * jnp.repeat(heights, dims[axis_at] // shards_of).reshape([-1 if axis == axis_at else 1 for axis in range(len(dims))])
    return gain


def noise(stream_key, extent, spread, reach, shards=(), held_as=jnp.bfloat16):
    drawn = spread * jax.random.normal(stream_key, extent, jnp.float32)
    if shards:
        drawn = drawn * levels(stream_key, extent, shards, -0.22, 0.18)
    return jnp.clip(drawn, -reach, reach).astype(held_as)


def setup_inputs(seed: int = 0) -> dict:
    arg_keys = jax.random.split(jax.random.key(seed), 6)
    return {
        "prognostic": noise(arg_keys[0], (FIELDS, LEV, NLON, NLAT), 1.0, 6.0, ((2, 4), (3, 8)), jnp.float32),
        "wind_zonal": jnp.clip(jax.random.uniform(arg_keys[1], (LEV, NLAT), jnp.float32, -1.0, 1.0) * levels(arg_keys[1], (LEV, NLAT), ((1, 8),), -0.4, 0.0), -1.0, 1.0),
        "wind_merid": jnp.clip(jax.random.uniform(arg_keys[2], (LEV, NLAT), jnp.float32, -0.5, 0.5) * levels(arg_keys[2], (LEV, NLAT), ((1, 8),), -0.4, 0.0), -0.5, 0.5),
        "layer_depth": jnp.clip(jnp.exp(jax.random.uniform(arg_keys[3], (LEV,), jnp.float32, math.log(0.25), math.log(1.0))), 0.25, 1.0),
        "diffusion": jnp.clip(jnp.exp(jax.random.uniform(arg_keys[4], (3, LEV), jnp.float32, math.log(0.05), math.log(0.4))), 0.05, 0.4),
    }


time_step = 0.15


def latitude(row_ids, lat_total):
    return (row_ids.astype(jnp.float32) + 0.5) * (math.pi / lat_total) - 0.5 * math.pi


def damping(row_ids, lat_total, circle_len):
    cos_ratio = jnp.cos(latitude(row_ids, lat_total)) / math.cos(0.25 * math.pi)
    wave_ids = jnp.arange(circle_len // 2 + 1)
    sine_vals = jnp.sin(wave_ids.astype(jnp.float32) * (math.pi / circle_len))
    safe_sines = jnp.where(wave_ids == 0, 1.0, sine_vals)
    return jnp.where(wave_ids[None, :] == 0, 1.0, jnp.minimum(1.0, cos_ratio[:, None] / safe_sines[None, :]))


def tendency(fields_now, north_rows, south_rows, east_cols, west_cols, row_ids, lat_total, wind_zonal, wind_merid, layer_depth, diffusion):
    latitudes = latitude(row_ids, lat_total)
    cos_centre = jnp.cos(latitudes)
    cos_north = jnp.cos(latitude(row_ids + 1, lat_total))
    cos_south = jnp.cos(latitude(row_ids - 1, lat_total))
    coriolis = jnp.sin(latitudes)
    zonal_diff = (east_cols - west_cols) / (2.0 * cos_centre)
    merid_diff = 0.5 * (north_rows - south_rows)
    advect = wind_zonal[:, None, :] * zonal_diff + wind_merid[:, None, :] * merid_diff
    diverge = zonal_diff[0] + (north_rows[1] * cos_north - south_rows[1] * cos_south) / (2.0 * cos_centre)
    zonal_tend = -advect[0] + coriolis * fields_now[1] - zonal_diff[2]
    merid_tend = -advect[1] - coriolis * fields_now[0] - merid_diff[2]
    height_tend = -advect[2] - layer_depth[:, None, None] * diverge
    tracer_tend = -advect[3:] + diffusion[:, :, None, None] * (north_rows[3:] - 2.0 * fields_now[3:] + south_rows[3:])
    return jnp.concatenate([zonal_tend[None], merid_tend[None], height_tend[None], tracer_tend], axis=0)


def reference(prognostic, wind_zonal, wind_merid, layer_depth, diffusion):
    row_ids = jnp.arange(NLAT)
    damp_table = jnp.transpose(damping(row_ids, NLAT, NLON))
    fields_now = prognostic
    for substep in range(ITERS):
        lat_padded = jnp.pad(fields_now, ((0, 0), (0, 0), (0, 0), (1, 1)))
        east_cols = jnp.roll(fields_now, -1, axis=2)
        west_cols = jnp.roll(fields_now, 1, axis=2)
        tendency_now = tendency(fields_now, lat_padded[:, :, :, 2:], lat_padded[:, :, :, :-2], east_cols, west_cols, row_ids, NLAT, wind_zonal, wind_merid, layer_depth, diffusion)
        spectrum = jnp.fft.rfft(tendency_now, axis=2)
        filtered = jnp.fft.irfft(spectrum * damp_table, n=NLON, axis=2)
        fields_now = fields_now + time_step * filtered
    return fields_now
```

```python
import math

import jax
import jax.numpy as jnp
import ml_dtypes
import numpy as np
from jax import lax
from jax.experimental import pallas as pl
from jax.experimental.pallas import tpu as pltpu
from jax.sharding import PartitionSpec as P

ITERS = 3


time_step = 0.15
highest = lax.Precision.HIGHEST


def with_halo(block, sides, width, periodic):
    for axis, dim in sides:
        count = lax.axis_size(axis)
        forward = [(i, i + 1) for i in range(count - 1)]
        if periodic:
            forward.append((count - 1, 0))
        backward = [(target, source) for source, target in forward]
        low = lax.ppermute(
            lax.slice_in_dim(block, block.shape[dim] - width, None, axis=dim), axis, forward
        )
        high = lax.ppermute(lax.slice_in_dim(block, 0, width, axis=dim), axis, backward)
        block = jnp.concatenate([low, block, high], axis=dim)
    return block


def latitude(row_ids, lat_total):
    return (row_ids.astype(jnp.float32) + 0.5) * (math.pi / lat_total) - 0.5 * math.pi


def damping(row_ids, lat_total, circle_len):
    cos_ratio = jnp.cos(latitude(row_ids, lat_total)) / math.cos(0.25 * math.pi)
    wave_ids = jnp.arange(circle_len // 2 + 1)
    sine_vals = jnp.sin(wave_ids.astype(jnp.float32) * (math.pi / circle_len))
    safe_sines = jnp.where(wave_ids == 0, 1.0, sine_vals)
    return jnp.where(
        wave_ids[None, :] == 0, 1.0, jnp.minimum(1.0, cos_ratio[:, None] / safe_sines[None, :])
    )


def tendency(
    fields_now,
    north_rows,
    south_rows,
    east_cols,
    west_cols,
    row_ids,
    lat_total,
    wind_zonal,
    wind_merid,
    layer_depth,
    diffusion,
):
    latitudes = latitude(row_ids, lat_total)
    cos_centre = jnp.cos(latitudes)
    cos_north = jnp.cos(latitude(row_ids + 1, lat_total))
    cos_south = jnp.cos(latitude(row_ids - 1, lat_total))
    coriolis = jnp.sin(latitudes)
    zonal_diff = (east_cols - west_cols) / (2.0 * cos_centre)
    merid_diff = 0.5 * (north_rows - south_rows)
    advect = wind_zonal[:, None, :] * zonal_diff + wind_merid[:, None, :] * merid_diff
    diverge = zonal_diff[0] + (north_rows[1] * cos_north - south_rows[1] * cos_south) / (
        2.0 * cos_centre
    )
    zonal_tend = -advect[0] + coriolis * fields_now[1] - zonal_diff[2]
    merid_tend = -advect[1] - coriolis * fields_now[0] - merid_diff[2]
    height_tend = -advect[2] - layer_depth[:, None, None] * diverge
    tracer_tend = -advect[3:] + diffusion[:, :, None, None] * (
        north_rows[3:] - 2.0 * fields_now[3:] + south_rows[3:]
    )
    return jnp.concatenate(
        [zonal_tend[None], merid_tend[None], height_tend[None], tracer_tend], axis=0
    )


def split_length(total):
    first = int(math.isqrt(total))
    while total % first != 0:
        first = first - 1
    return (first, total // first)


def trig_table(length):
    counts = jnp.arange(length, dtype=jnp.int32)
    phases = counts[:, None] * counts[None, :] % length
    angles = phases.astype(jnp.float32) * (2.0 * math.pi / length)
    return (jnp.cos(angles), jnp.sin(angles))


def twist_table(outer, inner, total):
    outer_ids = jnp.arange(outer, dtype=jnp.int32)
    inner_ids = jnp.arange(inner, dtype=jnp.int32)
    angles = (outer_ids[:, None] * inner_ids[None, :] % total).astype(jnp.float32) * (
        2.0 * math.pi / total
    )
    return (jnp.cos(angles)[None], jnp.sin(angles)[None])


def forward_real(signal):
    vectors, total = signal.shape
    inner, outer = split_length(total)
    grid = signal.reshape(vectors, outer, inner)
    cos_outer, sin_outer = trig_table(outer)
    first_re = jnp.einsum("mba,bk->mka", grid, cos_outer, precision=highest)
    first_im = -jnp.einsum("mba,bk->mka", grid, sin_outer, precision=highest)
    twist_cos, twist_sin = twist_table(outer, inner, total)
    mid_re = first_re * twist_cos + first_im * twist_sin
    mid_im = first_im * twist_cos - first_re * twist_sin
    cos_inner, sin_inner = trig_table(inner)
    last_re = jnp.einsum("mka,aq->mqk", mid_re, cos_inner, precision=highest) + jnp.einsum(
        "mka,aq->mqk", mid_im, sin_inner, precision=highest
    )
    last_im = jnp.einsum("mka,aq->mqk", mid_im, cos_inner, precision=highest) - jnp.einsum(
        "mka,aq->mqk", mid_re, sin_inner, precision=highest
    )
    return (last_re.reshape(vectors, total), last_im.reshape(vectors, total))


def inverse_real(spec_re, spec_im):
    vectors, total = spec_re.shape
    inner, outer = split_length(total)
    grid_re = spec_re.reshape(vectors, outer, inner)
    grid_im = spec_im.reshape(vectors, outer, inner)
    cos_outer, sin_outer = trig_table(outer)
    first_re = jnp.einsum("mba,bk->mka", grid_re, cos_outer, precision=highest) - jnp.einsum(
        "mba,bk->mka", grid_im, sin_outer, precision=highest
    )
    first_im = jnp.einsum("mba,bk->mka", grid_im, cos_outer, precision=highest) + jnp.einsum(
        "mba,bk->mka", grid_re, sin_outer, precision=highest
    )
    twist_cos, twist_sin = twist_table(outer, inner, total)
    mid_re = first_re * twist_cos - first_im * twist_sin
    mid_im = first_im * twist_cos + first_re * twist_sin
    cos_inner, sin_inner = trig_table(inner)
    last_re = jnp.einsum("mka,aq->mqk", mid_re, cos_inner, precision=highest) - jnp.einsum(
        "mka,aq->mqk", mid_im, sin_inner, precision=highest
    )
    return last_re.reshape(vectors, total)


def local(prognostic, wind_zonal, wind_merid, layer_depth, diffusion):
    field_count, level_count, col_count, row_count = prognostic.shape
    lat_devs = lax.axis_size("lat")
    lon_devs = lax.axis_size("lon")
    lat_total = row_count * lat_devs
    circle_len = col_count * lon_devs
    lat_pos = lax.axis_index("lat")
    lon_pos = lax.axis_index("lon")
    row_ids = lat_pos * row_count + jnp.arange(row_count, dtype=jnp.int32)
    quarter = lat_devs // 4
    is_polar = (lat_pos < quarter) | (lat_pos >= lat_devs - quarter)

    def smooth(sector, start_row):
        vectors, total, slab_rows = sector.shape
        halfway = damping(start_row + jnp.arange(slab_rows, dtype=jnp.int32), lat_total, circle_len)
        mirrored = halfway[:, 1 : circle_len // 2][:, ::-1]
        factors = jnp.concatenate([halfway, mirrored], axis=1)[None]
        rows_last = jnp.transpose(sector, (0, 2, 1)).reshape(vectors * slab_rows, total)
        spec_re, spec_im = forward_real(rows_last)
        spec_re = (spec_re.reshape(vectors, slab_rows, total) * factors).reshape(
            vectors * slab_rows, total
        )
        spec_im = (spec_im.reshape(vectors, slab_rows, total) * factors).reshape(
            vectors * slab_rows, total
        )
        back = inverse_real(spec_re, spec_im) * (1.0 / circle_len)
        return jnp.transpose(back.reshape(vectors, slab_rows, total), (0, 2, 1))

    fields_now = prognostic
    for substep in range(ITERS):
        lat_padded = with_halo(fields_now, (("lat", 3),), 1, False)
        lon_padded = with_halo(fields_now, (("lon", 2),), 1, True)
        tendency_now = tendency(
            fields_now,
            lat_padded[:, :, :, 2:],
            lat_padded[:, :, :, :-2],
            lon_padded[:, :, 2:],
            lon_padded[:, :, :-2],
            row_ids,
            lat_total,
            wind_zonal,
            wind_merid,
            layer_depth,
            diffusion,
        )
        flattened = tendency_now.reshape(field_count * level_count, col_count, row_count)

        def filter_sector(sector):
            slab_rows = sector.shape[2]
            start_row = lat_pos * row_count + lon_pos * slab_rows
            damped = lax.cond(
                is_polar, lambda inner: smooth(inner, start_row), lambda inner: inner, sector
            )
            return lax.all_to_all(damped, "lon", split_axis=1, concat_axis=2, tiled=True)

        filtered = filter_sector(
            lax.all_to_all(flattened, "lon", split_axis=2, concat_axis=1, tiled=True)
        )
        fields_now = fields_now + time_step * filtered.reshape(fields_now.shape)
    return fields_now


HALO = 3
SEG = 2 * HALO - 1
BLOCK = 32


def wave_layout(total):
    q = total // 4
    pad_a = -(-(q // 2 + 1) // 16) * 16
    wave_a = np.full(pad_a, -1)
    wave_a[: q // 2 + 1] = 4 * np.arange(q // 2 + 1)
    wave_b = 4 * np.arange(q // 2) + 2
    wave_c = 2 * np.arange(q) + 1
    return wave_a, wave_b, wave_c


def split_bf16(table):
    table = table.astype(np.float32)
    high = table.astype(ml_dtypes.bfloat16)
    low = (table - high.astype(np.float32)).astype(ml_dtypes.bfloat16)
    return np.stack([high, low])


def wave_tables(total):
    out_fwd, out_inv = [], []
    for waves, width in zip(wave_layout(total), (total // 4, total // 4, total // 2)):
        angle = 2 * np.pi * (waves[:, None] * np.arange(width)[None, :] % total) / total
        real = waves >= 0
        cos = np.where(real[:, None], np.cos(angle), 0.0)
        sin = np.where(real[:, None], np.sin(angle), 0.0)
        weight = np.where((waves == 0) | (2 * waves == total), 1.0, 2.0)[:, None] / total
        out_fwd.append(split_bf16(np.concatenate([cos, -sin], axis=0)))
        out_inv.append(split_bf16(np.concatenate([cos * weight, -sin * weight], axis=0).T))
    return out_fwd, out_inv


def wave_vectors(total):
    waves = np.concatenate(wave_layout(total))
    sigma = np.where(waves >= 0, np.sin(2 * np.pi * waves / total), 0.0)
    sine = np.where(waves > 0, np.sin(np.pi * waves / total), 1.0)
    inverse = np.where(waves == 0, 1e30, 1.0 / sine)
    return np.stack([sigma, inverse]).astype(np.float32)


def row_coefs(row_ids, lat_total, zonal, merid, depth, kappa, dyn):
    lat_c = latitude(row_ids, lat_total)
    cos_c = jnp.cos(lat_c)
    inv = 1.0 / cos_c
    cos_n = jnp.cos(latitude(row_ids + 1, lat_total))
    cos_s = jnp.cos(latitude(row_ids - 1, lat_total))
    ones = jnp.ones_like(cos_c)
    valid = ((row_ids >= 0) & (row_ids < lat_total)).astype(jnp.float32)
    depth = depth * dyn
    return dict(
        east=[-0.5 * merid + kappa[v] for v in range(3)],
        west=[0.5 * merid + kappa[v] for v in range(3)],
        mid=[-2.0 * kappa[v] * ones for v in range(3)],
        rot=dyn * jnp.sin(lat_c),
        grad=0.5 * dyn * ones,
        div_e=-0.5 * depth * cos_n * inv,
        div_w=0.5 * depth * cos_s * inv,
        adv=zonal * inv,
        pres=dyn * inv,
        cont=depth * inv,
        ratio=jnp.abs(cos_c) / math.cos(0.25 * math.pi),
        scale=time_step * valid,
    )


def main_coefs(c):
    return jnp.stack(
        c["east"] + c["west"] + c["mid"]
        + [c["rot"], c["grad"], c["div_e"], c["div_w"], c["adv"], c["pres"], c["cont"], c["ratio"], c["scale"]]
    )


def edge_coefs(c):
    def lay(a, b, d):
        parts = [jnp.zeros_like(c["rot"]) if p is None else p for p in (a, b, d)]
        return jnp.concatenate([jnp.pad(p, (0, BLOCK - p.shape[0])) for p in parts] + [jnp.zeros(128 - 3 * BLOCK)])

    return jnp.stack([
        lay(*c["east"]), lay(*c["west"]), lay(*c["mid"]),
        lay(c["rot"], None, None), lay(None, -c["rot"], None),
        lay(None, -c["grad"], None), lay(None, c["grad"], None),
        lay(None, None, c["div_e"]), lay(None, None, c["div_w"]),
        lay(c["adv"], c["adv"], c["adv"]), lay(c["pres"], None, c["cont"]),
        lay(c["ratio"], c["ratio"], c["ratio"]), lay(c["scale"], c["scale"], c["scale"]),
    ])


def substeps(state, edge, sigma, inv_sine, mc, ec):
    lane = lax.broadcasted_iota(jnp.int32, edge[0].shape, 1)
    first, last = lane == 0, lane == 127
    fac = mc(17) * jnp.minimum(1.0, mc(16) * inv_sine)
    efac = ec(12) * jnp.minimum(1.0, ec(11) * inv_sine)
    roll = lambda x, s: pltpu.roll(x, s % 128, 1)
    for step in range(ITERS):
        tends, zons, etend, ezon = [], [], None, None
        for part in range(2):
            a = [state[v][part] for v in range(3)]
            h = edge[part]
            east = [jnp.where(last, roll(h, 120 - BLOCK * v), roll(a[v], 127)) for v in range(3)]
            west = [jnp.where(first, roll(h, 126 - BLOCK * v), roll(a[v], 1)) for v in range(3)]
            t = [mc(v) * east[v] + mc(3 + v) * west[v] + mc(6 + v) * a[v] for v in range(3)]
            t[0] = t[0] + mc(9) * a[1]
            t[1] = t[1] - mc(9) * a[0] - mc(10) * (east[2] - west[2])
            t[2] = t[2] + mc(11) * east[1] + mc(12) * west[1]
            z = [mc(13) * a[v] for v in range(3)]
            z[0] = z[0] + mc(14) * a[2]
            z[2] = z[2] + mc(15) * a[0]
            tends.append(t)
            zons.append(z)
            if step < ITERS - 1:
                e = (
                    ec(0) * roll(h, 127) + ec(1) * roll(h, 1) + ec(2) * h
                    + ec(3) * roll(h, -BLOCK) + ec(4) * roll(h, BLOCK)
                    + ec(5) * roll(h, -BLOCK - 1) + ec(6) * roll(h, -BLOCK + 1)
                    + ec(7) * roll(h, BLOCK - 1) + ec(8) * roll(h, BLOCK + 1)
                )
                ze = ec(9) * h + ec(10) * roll(h, 64)
                if part == 0:
                    etend, ezon = [e], [ze]
                else:
                    etend.append(e)
                    ezon.append(ze)
        state = [
            (
                state[v][0] + fac * (tends[0][v] + sigma * zons[1][v]),
                state[v][1] + fac * (tends[1][v] - sigma * zons[0][v]),
            )
            for v in range(3)
        ]
        if step < ITERS - 1:
            edge = (
                edge[0] + efac * (etend[0] + sigma * ezon[1]),
                edge[1] + efac * (etend[1] - sigma * ezon[0]),
            )
    return state


def wave_kernel(x_ref, e_ref, mc_ref, ec_ref, kv_ref, fa, fb, fc, ia, ib, ic, out_ref, xh, xl, sre, sim, sh, sl):
    quarter = x_ref.shape[2]
    ka, kb, kc = fa.shape[1] // 2, fb.shape[1] // 2, fc.shape[1] // 2
    waves = ka + kb + kc
    rows = 16

    @pl.loop(0, quarter // rows)
    def _(i):
        at = pl.ds(pl.multiple_of(i * rows, rows), rows)
        for tile in range(4):
            lanes = slice(tile * 128, tile * 128 + 128)
            x = [x_ref[s, tile, at, :] if tile < 3 else e_ref[s, at, :] for s in range(4)]
            y0, y1 = x[0] + x[2], x[1] + x[3]
            for part, val in enumerate((y0 + y1, y0 - y1, x[0] - x[2], x[1] - x[3])):
                high = val.astype(jnp.bfloat16)
                to = pl.ds(pl.multiple_of(part * quarter + i * rows, rows), rows)
                xh[to, lanes] = high
                xl[to, lanes] = (val - high.astype(jnp.float32)).astype(jnp.bfloat16)

    def mul(table, at, high, low):
        dot = lambda p, q: jnp.dot(p, q, preferred_element_type=jnp.float32)
        top = table[0, at, :]
        return dot(top, high) + dot(table[1, at, :], high) + dot(top, low)

    for table, half, base, start, size in (
        (fa, ka, 0, 0, quarter), (fb, kb, ka, quarter, quarter), (fc, kc, ka + kb, 2 * quarter, 2 * quarter)
    ):
        src = slice(start, start + size)
        piece = half if half <= 304 else half // 2
        for p in range(0, half, piece):
            sre[base + p : base + p + piece, :] = mul(table, slice(p, p + piece), xh[src, :], xl[src, :])
            sim[base + p : base + p + piece, :] = mul(table, slice(half + p, half + p + piece), xh[src, :], xl[src, :])

    @pl.loop(0, waves // rows)
    def _(i):
        highs = [[None] * 2 for _ in range(3)]
        lows = [[None] * 2 for _ in range(3)]
        parts = []
        for sub in range(2):
            at = pl.ds(pl.multiple_of(i * rows + sub * 8, 8), 8)
            take = lambda tile: (sre[at, tile * 128 : tile * 128 + 128], sim[at, tile * 128 : tile * 128 + 128])
            mc = lambda r: mc_ref[r : r + 1, :]
            ec = lambda r: ec_ref[r : r + 1, :]
            parts.append(substeps([take(0), take(1), take(2)], take(3), kv_ref[0, at, :], kv_ref[1, at, :], mc, ec))
        at = pl.ds(pl.multiple_of(i * rows, rows), rows)
        for v in range(3):
            for part in range(2):
                val = jnp.concatenate([parts[0][v][part], parts[1][v][part]], axis=0)
                high = val.astype(jnp.bfloat16)
                sh[part, at, v * 128 : v * 128 + 128] = high
                sl[part, at, v * 128 : v * 128 + 128] = (val - high.astype(jnp.float32)).astype(jnp.bfloat16)

    def inv(table, base, half, at):
        dot = lambda p, q: jnp.dot(p, q, preferred_element_type=jnp.float32)
        total = None
        for part in range(2):
            cols = slice(part * half, part * half + half)
            high = sh[part, base : base + half, :]
            low = sl[part, base : base + half, :]
            term = dot(table[0, at, cols], high) + dot(table[1, at, cols], high) + dot(table[0, at, cols], low)
            total = term if total is None else total + term
        return total

    piece = 192
    for p in range(0, quarter, piece):
        at = slice(p, p + piece)
        ya = inv(ia, 0, ka, at)
        yb = inv(ib, ka, kb, at)
        y0, y1 = ya + yb, ya - yb
        o0 = inv(ic, ka + kb, kc, at)
        o1 = inv(ic, ka + kb, kc, slice(quarter + p, quarter + p + piece))
        for v in range(3):
            lanes = slice(v * 128, v * 128 + 128)
            out_ref[0, v, at, :] = (y0 + o0)[:, lanes]
            out_ref[1, v, at, :] = (y1 + o1)[:, lanes]
            out_ref[2, v, at, :] = (y0 - o0)[:, lanes]
            out_ref[3, v, at, :] = (y1 - o1)[:, lanes]


def lat_shift(block, count, up):
    pairs = [(i, i + 1) for i in range(count - 1)]
    return lax.ppermute(block, "lat", pairs if up else [(b, a) for a, b in pairs])


def local_waves(prognostic, wind_zonal, wind_merid, layer_depth, diffusion):
    field_count, level_count, col_count, row_count = prognostic.shape
    lat_devs = lax.axis_size("lat")
    lat_total = row_count * lat_devs
    total = col_count * 4
    lat_pos, lon_pos = lax.axis_index("lat"), lax.axis_index("lon")
    level = lon_pos % 2
    dyn = (lon_pos < 2).astype(jnp.float32)

    winds = jnp.stack([wind_zonal, wind_merid])
    winds_low = lat_shift(winds[:, :, -HALO:], lat_devs, True)
    winds_high = lat_shift(winds[:, :, :HALO], lat_devs, False)
    keep = HALO - 1
    winds_edge = jnp.concatenate([winds_low, winds[:, :, :keep], winds[:, :, -keep:], winds_high], axis=2)
    pick = lambda a, axis: lax.dynamic_index_in_dim(a, level, axis, keepdims=False)
    depth = pick(layer_depth, 0)
    kappa = pick(diffusion, 1) * (1.0 - dyn)
    row_ids = lat_pos * row_count + jnp.arange(row_count, dtype=jnp.int32)
    offsets = np.concatenate([np.arange(-HALO, keep), np.arange(-keep, HALO) + row_count]).astype(np.int32)
    edge_ids = lat_pos * row_count + jnp.asarray(offsets)
    w_main, w_edge = pick(winds, 1), pick(winds_edge, 1)
    mc = main_coefs(row_coefs(row_ids, lat_total, w_main[0], w_main[1], depth, kappa, dyn))
    ec = edge_coefs(row_coefs(edge_ids, lat_total, w_edge[0], w_edge[1], depth, kappa, dyn))

    grouped = prognostic.reshape(2, 3, 2, col_count, row_count).transpose(0, 2, 1, 3, 4)
    grouped = grouped.reshape(4, 3, col_count, row_count)
    circles = lax.all_to_all(grouped, "lon", split_axis=0, concat_axis=0, tiled=True)
    low = lat_shift(circles[..., -HALO:].transpose(3, 0, 1, 2), lat_devs, True)
    high = lat_shift(circles[..., :HALO].transpose(3, 0, 1, 2), lat_devs, False)
    edge = jnp.concatenate(
        [low.transpose(1, 2, 3, 0), circles[..., :keep], circles[..., -keep:], high.transpose(1, 2, 3, 0)], axis=3
    )
    edge = jnp.pad(edge, ((0, 0), (0, 0), (0, 0), (0, BLOCK - 2 * SEG)))
    edge = edge.transpose(0, 2, 1, 3).reshape(4, col_count, 3 * BLOCK)
    edge = jnp.pad(edge, ((0, 0), (0, 0), (0, 128 - 3 * BLOCK)))

    fwd, bwd = wave_tables(total)
    vectors = wave_vectors(total)
    waves = vectors.shape[1]
    vectors = jnp.broadcast_to(jnp.asarray(vectors)[:, :, None], (2, waves, 128))
    back = pl.pallas_call(
        wave_kernel,
        out_shape=jax.ShapeDtypeStruct(circles.shape, jnp.float32),
        in_specs=[pl.BlockSpec(memory_space=pltpu.VMEM)] * 11,
        out_specs=pl.BlockSpec(memory_space=pltpu.VMEM),
        scratch_shapes=[
            pltpu.VMEM((total, 512), jnp.bfloat16),
            pltpu.VMEM((total, 512), jnp.bfloat16),
            pltpu.VMEM((waves, 512), jnp.float32),
            pltpu.VMEM((waves, 512), jnp.float32),
            pltpu.VMEM((2, waves, 384), jnp.bfloat16),
            pltpu.VMEM((2, waves, 384), jnp.bfloat16),
        ],
        compiler_params=pltpu.CompilerParams(vmem_limit_bytes=58 * 2**20),
        name="waves",
    )(circles, edge, mc, ec, vectors, *[jnp.asarray(t) for t in fwd + bwd])
    home = lax.all_to_all(back, "lon", split_axis=0, concat_axis=0, tiled=True)
    home = home.reshape(2, 2, 3, col_count, row_count).transpose(0, 2, 1, 3, 4)
    return home.reshape(prognostic.shape)


def solution(mesh):
    return jax.shard_map(
        local_waves if mesh.shape["lon"] == 4 else local,
        mesh=mesh,
        in_specs=(P(None, None, "lon", "lat"), P(None, "lat"), P(None, "lat"), P(), P()),
        out_specs=P(None, None, "lon", "lat"),
        check_vma=False,
    )
```

```python
import math

import jax
import jax.numpy as jnp
import ml_dtypes
import numpy as np
from jax import lax
from jax.experimental import pallas as pl
from jax.experimental.pallas import tpu as pltpu
from jax.sharding import PartitionSpec as P

ITERS = 3


time_step = 0.15
highest = lax.Precision.HIGHEST


def with_halo(block, sides, width, periodic):
    for axis, dim in sides:
        count = lax.axis_size(axis)
        forward = [(i, i + 1) for i in range(count - 1)]
        if periodic:
            forward.append((count - 1, 0))
        backward = [(target, source) for source, target in forward]
        low = lax.ppermute(
            lax.slice_in_dim(block, block.shape[dim] - width, None, axis=dim), axis, forward
        )
        high = lax.ppermute(lax.slice_in_dim(block, 0, width, axis=dim), axis, backward)
        block = jnp.concatenate([low, block, high], axis=dim)
    return block


def latitude(row_ids, lat_total):
    return (row_ids.astype(jnp.float32) + 0.5) * (math.pi / lat_total) - 0.5 * math.pi


def damping(row_ids, lat_total, circle_len):
    cos_ratio = jnp.cos(latitude(row_ids, lat_total)) / math.cos(0.25 * math.pi)
    wave_ids = jnp.arange(circle_len // 2 + 1)
    sine_vals = jnp.sin(wave_ids.astype(jnp.float32) * (math.pi / circle_len))
    safe_sines = jnp.where(wave_ids == 0, 1.0, sine_vals)
    return jnp.where(
        wave_ids[None, :] == 0, 1.0, jnp.minimum(1.0, cos_ratio[:, None] / safe_sines[None, :])
    )


def tendency(
    fields_now,
    north_rows,
    south_rows,
    east_cols,
    west_cols,
    row_ids,
    lat_total,
    wind_zonal,
    wind_merid,
    layer_depth,
    diffusion,
):
    latitudes = latitude(row_ids, lat_total)
    cos_centre = jnp.cos(latitudes)
    cos_north = jnp.cos(latitude(row_ids + 1, lat_total))
    cos_south = jnp.cos(latitude(row_ids - 1, lat_total))
    coriolis = jnp.sin(latitudes)
    zonal_diff = (east_cols - west_cols) / (2.0 * cos_centre)
    merid_diff = 0.5 * (north_rows - south_rows)
    advect = wind_zonal[:, None, :] * zonal_diff + wind_merid[:, None, :] * merid_diff
    diverge = zonal_diff[0] + (north_rows[1] * cos_north - south_rows[1] * cos_south) / (
        2.0 * cos_centre
    )
    zonal_tend = -advect[0] + coriolis * fields_now[1] - zonal_diff[2]
    merid_tend = -advect[1] - coriolis * fields_now[0] - merid_diff[2]
    height_tend = -advect[2] - layer_depth[:, None, None] * diverge
    tracer_tend = -advect[3:] + diffusion[:, :, None, None] * (
        north_rows[3:] - 2.0 * fields_now[3:] + south_rows[3:]
    )
    return jnp.concatenate(
        [zonal_tend[None], merid_tend[None], height_tend[None], tracer_tend], axis=0
    )


def split_length(total):
    first = int(math.isqrt(total))
    while total % first != 0:
        first = first - 1
    return (first, total // first)


def trig_table(length):
    counts = jnp.arange(length, dtype=jnp.int32)
    phases = counts[:, None] * counts[None, :] % length
    angles = phases.astype(jnp.float32) * (2.0 * math.pi / length)
    return (jnp.cos(angles), jnp.sin(angles))


def twist_table(outer, inner, total):
    outer_ids = jnp.arange(outer, dtype=jnp.int32)
    inner_ids = jnp.arange(inner, dtype=jnp.int32)
    angles = (outer_ids[:, None] * inner_ids[None, :] % total).astype(jnp.float32) * (
        2.0 * math.pi / total
    )
    return (jnp.cos(angles)[None], jnp.sin(angles)[None])


def forward_real(signal):
    vectors, total = signal.shape
    inner, outer = split_length(total)
    grid = signal.reshape(vectors, outer, inner)
    cos_outer, sin_outer = trig_table(outer)
    first_re = jnp.einsum("mba,bk->mka", grid, cos_outer, precision=highest)
    first_im = -jnp.einsum("mba,bk->mka", grid, sin_outer, precision=highest)
    twist_cos, twist_sin = twist_table(outer, inner, total)
    mid_re = first_re * twist_cos + first_im * twist_sin
    mid_im = first_im * twist_cos - first_re * twist_sin
    cos_inner, sin_inner = trig_table(inner)
    last_re = jnp.einsum("mka,aq->mqk", mid_re, cos_inner, precision=highest) + jnp.einsum(
        "mka,aq->mqk", mid_im, sin_inner, precision=highest
    )
    last_im = jnp.einsum("mka,aq->mqk", mid_im, cos_inner, precision=highest) - jnp.einsum(
        "mka,aq->mqk", mid_re, sin_inner, precision=highest
    )
    return (last_re.reshape(vectors, total), last_im.reshape(vectors, total))


def inverse_real(spec_re, spec_im):
    vectors, total = spec_re.shape
    inner, outer = split_length(total)
    grid_re = spec_re.reshape(vectors, outer, inner)
    grid_im = spec_im.reshape(vectors, outer, inner)
    cos_outer, sin_outer = trig_table(outer)
    first_re = jnp.einsum("mba,bk->mka", grid_re, cos_outer, precision=highest) - jnp.einsum(
        "mba,bk->mka", grid_im, sin_outer, precision=highest
    )
    first_im = jnp.einsum("mba,bk->mka", grid_im, cos_outer, precision=highest) + jnp.einsum(
        "mba,bk->mka", grid_re, sin_outer, precision=highest
    )
    twist_cos, twist_sin = twist_table(outer, inner, total)
    mid_re = first_re * twist_cos - first_im * twist_sin
    mid_im = first_im * twist_cos + first_re * twist_sin
    cos_inner, sin_inner = trig_table(inner)
    last_re = jnp.einsum("mka,aq->mqk", mid_re, cos_inner, precision=highest) - jnp.einsum(
        "mka,aq->mqk", mid_im, sin_inner, precision=highest
    )
    return last_re.reshape(vectors, total)


def local(prognostic, wind_zonal, wind_merid, layer_depth, diffusion):
    field_count, level_count, col_count, row_count = prognostic.shape
    lat_devs = lax.axis_size("lat")
    lon_devs = lax.axis_size("lon")
    lat_total = row_count * lat_devs
    circle_len = col_count * lon_devs
    lat_pos = lax.axis_index("lat")
    lon_pos = lax.axis_index("lon")
    row_ids = lat_pos * row_count + jnp.arange(row_count, dtype=jnp.int32)
    quarter = lat_devs // 4
    is_polar = (lat_pos < quarter) | (lat_pos >= lat_devs - quarter)

    def smooth(sector, start_row):
        vectors, total, slab_rows = sector.shape
        halfway = damping(start_row + jnp.arange(slab_rows, dtype=jnp.int32), lat_total, circle_len)
        mirrored = halfway[:, 1 : circle_len // 2][:, ::-1]
        factors = jnp.concatenate([halfway, mirrored], axis=1)[None]
        rows_last = jnp.transpose(sector, (0, 2, 1)).reshape(vectors * slab_rows, total)
        spec_re, spec_im = forward_real(rows_last)
        spec_re = (spec_re.reshape(vectors, slab_rows, total) * factors).reshape(
            vectors * slab_rows, total
        )
        spec_im = (spec_im.reshape(vectors, slab_rows, total) * factors).reshape(
            vectors * slab_rows, total
        )
        back = inverse_real(spec_re, spec_im) * (1.0 / circle_len)
        return jnp.transpose(back.reshape(vectors, slab_rows, total), (0, 2, 1))

    fields_now = prognostic
    for substep in range(ITERS):
        lat_padded = with_halo(fields_now, (("lat", 3),), 1, False)
        lon_padded = with_halo(fields_now, (("lon", 2),), 1, True)
        tendency_now = tendency(
            fields_now,
            lat_padded[:, :, :, 2:],
            lat_padded[:, :, :, :-2],
            lon_padded[:, :, 2:],
            lon_padded[:, :, :-2],
            row_ids,
            lat_total,
            wind_zonal,
            wind_merid,
            layer_depth,
            diffusion,
        )
        flattened = tendency_now.reshape(field_count * level_count, col_count, row_count)

        def filter_sector(sector):
            slab_rows = sector.shape[2]
            start_row = lat_pos * row_count + lon_pos * slab_rows
            damped = lax.cond(
                is_polar, lambda inner: smooth(inner, start_row), lambda inner: inner, sector
            )
            return lax.all_to_all(damped, "lon", split_axis=1, concat_axis=2, tiled=True)

        filtered = filter_sector(
            lax.all_to_all(flattened, "lon", split_axis=2, concat_axis=1, tiled=True)
        )
        fields_now = fields_now + time_step * filtered.reshape(fields_now.shape)
    return fields_now


HALO = 3
BLOCK = 32
FOLD = 8
MESH = pl.DeviceIdType.MESH


def wave_layout(total):
    q = total // 4
    pad_a = -(-(q // 2 + 1) // 32) * 32
    wave_a = np.full(pad_a, -1)
    wave_a[: q // 2 + 1] = 4 * np.arange(q // 2 + 1)
    wave_b = 4 * np.arange(q // 2) + 2
    wave_c = 2 * np.arange(q) + 1
    return wave_a, wave_b, wave_c


def split_bf16(table):
    table = table.astype(np.float32)
    high = table.astype(ml_dtypes.bfloat16)
    low = (table - high.astype(np.float32)).astype(ml_dtypes.bfloat16)
    return np.stack([high, low])


def wave_tables(total):
    out_fwd, out_inv = [], []
    for waves, width in zip(wave_layout(total), (total // 4, total // 4, total // 2)):
        angle = 2 * np.pi * (waves[:, None] * np.arange(width)[None, :] % total) / total
        real = waves >= 0
        cos = np.where(real[:, None], np.cos(angle), 0.0)
        sin = np.where(real[:, None], np.sin(angle), 0.0)
        weight = np.where((waves == 0) | (2 * waves == total), 1.0, 2.0)[:, None] / total
        out_fwd.append(split_bf16(np.concatenate([cos, -sin], axis=0)))
        out_inv.append(split_bf16(np.concatenate([cos * weight, -sin * weight], axis=0).T))
    return out_fwd, out_inv


def wave_vectors(total):
    waves = np.concatenate(wave_layout(total))
    sigma = np.where(waves >= 0, np.sin(2 * np.pi * waves / total), 0.0)
    sine = np.where(waves > 0, np.sin(np.pi * waves / total), 1.0)
    inverse = np.where(waves == 0, 1e30, 1.0 / sine)
    return np.stack([sigma, inverse]).astype(np.float32)


def geometry(row_ids, lat_total):
    def lat(ids):
        step = np.float32(math.pi / lat_total)
        return ((ids.astype(np.float32) + np.float32(0.5)) * step - np.float32(0.5 * math.pi)).astype(np.float64)

    cos_c = np.cos(lat(row_ids))
    valid = (row_ids >= 0) & (row_ids < lat_total)
    rows = [
        1.0 / cos_c,
        np.sin(lat(row_ids)),
        0.5 * np.cos(lat(row_ids + 1)) / cos_c,
        0.5 * np.cos(lat(row_ids - 1)) / cos_c,
        np.abs(cos_c) / math.cos(0.25 * math.pi),
        np.where(valid, time_step, 0.0),
    ]
    return np.stack(rows + [np.zeros_like(cos_c)] * 2).astype(np.float32)


def geometry_tables(lat_devs, row_count):
    total = lat_devs * row_count
    mains, edges = [], []
    keep = HALO - 1
    offsets = np.concatenate([np.arange(-HALO, keep), np.arange(-keep, HALO) + row_count])
    for pos in range(lat_devs):
        mains.append(geometry(pos * row_count + np.arange(row_count), total))
        short = geometry(pos * row_count + offsets, total)
        wide = np.zeros((8, 128), np.float32)
        for v in range(3):
            wide[:, BLOCK * v : BLOCK * v + len(offsets)] = short
        edges.append(wide)
    return np.stack(mains), np.stack(edges)


def roll(x, shift):
    return pltpu.roll(x, shift % 128, 1)


def substeps(state, edge, sigma, inv_sine, mc, ec):
    lane = lax.broadcasted_iota(jnp.int32, edge[0].shape, 1)
    first, last = lane == 0, lane == 127
    fac = mc(17) * jnp.minimum(1.0, mc(16) * inv_sine)
    efac = ec(12) * jnp.minimum(1.0, ec(11) * inv_sine)
    for step in range(ITERS):
        tends, zons, etend, ezon = [], [], [], []
        for part in range(2):
            a = [state[v][part] for v in range(3)]
            h = edge[part]
            east = [jnp.where(last, roll(h, 120 - BLOCK * v), roll(a[v], 127)) for v in range(3)]
            west = [jnp.where(first, roll(h, 126 - BLOCK * v), roll(a[v], 1)) for v in range(3)]
            t = [mc(v) * east[v] + mc(3 + v) * west[v] + mc(6 + v) * a[v] for v in range(3)]
            t[0] = t[0] + mc(9) * a[1]
            t[1] = t[1] - mc(9) * a[0] - mc(10) * (east[2] - west[2])
            t[2] = t[2] + mc(11) * east[1] + mc(12) * west[1]
            z = [mc(13) * a[v] for v in range(3)]
            z[0] = z[0] + mc(14) * a[2]
            z[2] = z[2] + mc(15) * a[0]
            tends.append(t)
            zons.append(z)
            if step < ITERS - 1:
                etend.append(
                    ec(0) * roll(h, 127) + ec(1) * roll(h, 1) + ec(2) * h
                    + ec(3) * roll(h, -BLOCK) + ec(4) * roll(h, BLOCK)
                    + ec(5) * roll(h, -BLOCK - 1) + ec(6) * roll(h, -BLOCK + 1)
                    + ec(7) * roll(h, BLOCK - 1) + ec(8) * roll(h, BLOCK + 1)
                )
                ezon.append(ec(9) * h + ec(10) * roll(h, 64))
        state = [
            (
                state[v][0] + fac * (tends[0][v] + sigma * zons[1][v]),
                state[v][1] + fac * (tends[1][v] - sigma * zons[0][v]),
            )
            for v in range(3)
        ]
        if step < ITERS - 1:
            edge = (
                edge[0] + efac * (etend[0] + sigma * ezon[1]),
                edge[1] + efac * (etend[1] - sigma * ezon[0]),
            )
    return state


def wave_kernel(
    x_ref, wz_ref, wm_ref, depth_ref, kappa_ref, gm_ref, ge_ref, kv_ref,
    fa_h, fb_h, fc_h, ia_h, ib_h, ic_h, out_ref,
    fa, fb, fc, ia, ib, ic, recv, home, xh, xl, xs, sre, sim, sh, sl, ss,
    wind, wind_in, up, down, from_low, from_high, mc_ref, ec_ref,
    table_sem, own_sem, go_send, go_recv, back_send, back_recv, wind_send, wind_recv, edge_send, edge_recv,
):
    lat, lon = lax.axis_index("lat"), lax.axis_index("lon")
    lat_devs = lax.axis_size("lat")
    quarter = recv.shape[2]
    ka, kb, kc = fa.shape[1] // 2, fb.shape[1] // 2, fc.shape[1] // 2
    waves = ka + kb + kc
    has_low, has_high = lat > 0, lat < lat_devs - 1
    kind, level = lon // 2, lon % 2

    barrier = pltpu.get_barrier_semaphore()
    for p in (1, 2, 3):
        pl.semaphore_signal(barrier, inc=1, device_id=(lat, (lon + p) % 4), device_id_type=MESH)

    @pl.when(has_low)
    def _():
        pl.semaphore_signal(barrier, inc=1, device_id=(lat - 1, lon), device_id_type=MESH)

    @pl.when(has_high)
    def _():
        pl.semaphore_signal(barrier, inc=1, device_id=(lat + 1, lon), device_id_type=MESH)

    pl.semaphore_wait(barrier, 3 + jnp.where(has_low, 1, 0) + jnp.where(has_high, 1, 0))

    def go(p, v):
        to = (lon + p) % 4
        return pltpu.make_async_remote_copy(
            src_ref=x_ref.at[3 * (to // 2) + v, to % 2], dst_ref=recv.at[p, v],
            send_sem=go_send.at[p, v], recv_sem=go_recv.at[p, v],
            device_id=(lat, to), device_id_type=MESH,
        )

    def back(p, v):
        to = (lon + p) % 4
        return pltpu.make_async_remote_copy(
            src_ref=home.at[to, v], dst_ref=out_ref.at[3 * kind + v, level],
            send_sem=back_send.at[p, v], recv_sem=back_recv.at[p, v],
            device_id=(lat, to), device_id_type=MESH,
        )

    def own_in(v):
        return pltpu.make_async_copy(x_ref.at[3 * kind + v, level], recv.at[0, v], own_sem.at[0, v])

    def own_out(v):
        return pltpu.make_async_copy(home.at[lon, v], out_ref.at[3 * kind + v, level], own_sem.at[1, v])

    def beside(src, dst, side, send_sem, recv_sem):
        return pltpu.make_async_remote_copy(
            src_ref=src, dst_ref=dst, send_sem=send_sem.at[side], recv_sem=recv_sem.at[side],
            device_id=((lat + (1 if side == 0 else lat_devs - 1)) % lat_devs, lon), device_id_type=MESH,
        )

    for v in range(3):
        for p in (2, 1, 3):
            go(p, v).start()
        own_in(v).start()
    tables = [
        pltpu.make_async_copy(src, dst, table_sem.at[i])
        for i, (src, dst) in enumerate(
            ((fa_h, fa), (fb_h, fb), (fc_h, fc), (ia_h, ia), (ib_h, ib), (ic_h, ic))
        )
    ]
    for t in tables:
        t.start()

    wind[0:2, :] = wz_ref[...]
    wind[2:4, :] = wm_ref[...]
    wind[4:8, :] = jnp.zeros((4, 128), jnp.float32)
    up_wind = lambda: beside(wind, wind_in.at[0], 0, wind_send, wind_recv)
    down_wind = lambda: beside(wind, wind_in.at[1], 1, wind_send, wind_recv)
    up_edge = lambda: beside(up, from_low, 0, edge_send, edge_recv)
    down_edge = lambda: beside(down, from_high, 1, edge_send, edge_recv)

    @pl.when(has_high)
    def _():
        up_wind().start()

    @pl.when(has_low)
    def _():
        down_wind().start()

    @pl.when(jnp.logical_not(has_low))
    def _():
        wind_in[0] = jnp.zeros((8, 128), jnp.float32)
        from_low[...] = jnp.zeros(from_low.shape, jnp.float32)

    @pl.when(jnp.logical_not(has_high))
    def _():
        wind_in[1] = jnp.zeros((8, 128), jnp.float32)
        from_high[...] = jnp.zeros(from_high.shape, jnp.float32)

    @pl.when(has_high)
    def _():
        up_wind().wait_send()
        down_wind().wait_recv()

    @pl.when(has_low)
    def _():
        down_wind().wait_send()
        up_wind().wait_recv()

    lane8 = lax.broadcasted_iota(jnp.int32, (8, 128), 1)
    spot8, block8 = lane8 % BLOCK, lane8 // BLOCK
    dyn = jnp.where(lon < 2, 1.0, 0.0).astype(jnp.float32)
    depth = depth_ref[level] * dyn
    kappa = [kappa_ref[v, level] * (1.0 - dyn) for v in range(3)]
    row = lambda ref, r: ref[lat, r : r + 1, :]
    wz, wm = wind[pl.ds(level, 1), :], wind[pl.ds(2 + level, 1), :]
    one = jnp.ones((1, 128), jnp.float32)
    inv, rot, cn, cs = (row(gm_ref, r) for r in range(4))
    coefs = (
        [kappa[v] - 0.5 * wm for v in range(3)] + [kappa[v] + 0.5 * wm for v in range(3)]
        + [-2.0 * kappa[v] * one for v in range(3)]
        + [dyn * rot, 0.5 * dyn * one, -depth * cn, depth * cs, wz * inv, dyn * inv, depth * inv, row(gm_ref, 4), row(gm_ref, 5)]
    )
    for r, c in enumerate(coefs):
        mc_ref[r : r + 1, :] = c

    below = jnp.where(lane8 >= 128 - HALO, wind_in[0], wind[...])
    above = jnp.where(lane8 < HALO, wind_in[1], wind[...])
    ewind = jnp.zeros((8, 128), jnp.float32)
    for v in range(3):
        val = jnp.where(spot8 < 5, roll(below, BLOCK * v + 3), roll(above, BLOCK * v + 7))
        ewind = jnp.where(block8 == v, val, ewind)
    used = (spot8 < 10) & (block8 < 3)
    ewind = jnp.where(used, ewind, 0.0)
    ec_ref[0:8, :] = ewind
    ez, em = ec_ref[pl.ds(level, 1), :], ec_ref[pl.ds(2 + level, 1), :]
    block = block8[0:1]
    only = lambda v, val: jnp.where(block == v, val, 0.0)
    ekap = only(0, kappa[0] * one) + only(1, kappa[1] * one) + only(2, kappa[2] * one)
    inv, rot, cn, cs = (row(ge_ref, r) for r in range(4))
    coefs = [
        ekap - 0.5 * em, ekap + 0.5 * em, -2.0 * ekap,
        only(0, dyn * rot), only(1, -dyn * rot), only(1, -0.5 * dyn * one), only(1, 0.5 * dyn * one),
        only(2, -depth * cn), only(2, depth * cs), ez * inv, only(0, dyn * inv) + only(2, depth * inv),
        row(ge_ref, 4), row(ge_ref, 5),
    ]
    for r, c in enumerate(coefs):
        ec_ref[r : r + 1, :] = c

    rows = 16
    slots = [(lon - s + 4) % 4 for s in range(4)]

    def split_in(v):
        @pl.loop(0, quarter // rows)
        def _(i):
            at = pl.ds(pl.multiple_of(i * rows, rows), rows)
            x = [recv[slots[s], v, at, :] for s in range(4)]
            y0, y1 = x[0] + x[2], x[1] + x[3]
            for part, val in enumerate((y0 + y1, y0 - y1, x[0] - x[2], x[1] - x[3])):
                high = val.astype(jnp.bfloat16)
                low = (val - high.astype(jnp.float32)).astype(jnp.bfloat16)
                to = pl.ds(pl.multiple_of(part * quarter + i * rows, rows), rows)
                if v < 2:
                    xh[to, v * 128 : v * 128 + 128] = high
                    xl[to, v * 128 : v * 128 + 128] = low
                else:
                    xs[to, 0:128] = high
                    xs[to, 128:256] = low

    dot = lambda p, q: jnp.dot(p, q, preferred_element_type=jnp.float32)

    def pair(top, bottom, high, low):
        return dot(top, high) + dot(bottom, high) + dot(top, low)

    def single(top, bottom, both):
        full = dot(top, both)
        return full[:, :128] + full[:, 128:] + dot(bottom, both[:, :128])

    def forward(lanes, product):
        for table, half, base, start, size in (
            (fa, ka, 0, 0, quarter), (fb, kb, ka, quarter, quarter), (fc, kc, ka + kb, 2 * quarter, 2 * quarter)
        ):
            src = slice(start, start + size)
            piece = half if half <= 320 else half // 2
            for dest, shift in ((sre, 0), (sim, half)):
                for p in range(0, half, piece):
                    at = slice(shift + p, shift + p + piece)
                    dest[base + p : base + p + piece, lanes] = product(table[0, at, :], table[1, at, :], src)

    def arrived(v):
        for p in (1, 2, 3):
            go(p, v).wait_recv()
        own_in(v).wait()

    arrived(0)
    split_in(0)
    arrived(1)
    split_in(1)
    for t in tables[:3]:
        t.wait()
    forward(slice(0, 256), lambda top, bottom, src: pair(top, bottom, xh[src, :], xl[src, :]))
    arrived(2)
    split_in(2)
    forward(slice(256, 384), lambda top, bottom, src: single(top, bottom, xs[src, :]))

    lane = lax.broadcasted_iota(jnp.int32, (8, 128), 1)
    spot, blk = lane % BLOCK, lane // BLOCK
    span = 4 * FOLD

    @pl.loop(0, waves // span)
    def _(i):
        ups = jnp.zeros((8, 128), jnp.float32)
        downs = ups
        for f in range(FOLD):
            at = pl.ds(pl.multiple_of(i * span + (f // 2) * 8, 8), 8)
            src = (sre, sim)[f % 2]
            here = (spot >= 3 * f) & (spot < 3 * f + 3)
            for v in range(3):
                a = src[at, v * 128 : v * 128 + 128]
                mask = here & (blk == v)
                ups = jnp.where(mask, roll(a, BLOCK * v + 3 * f + 3), ups)
                downs = jnp.where(mask, roll(a, BLOCK * v + 3 * f), downs)
        to = pl.ds(pl.multiple_of(i * 8, 8), 8)
        up[to, :] = ups
        down[to, :] = downs

    @pl.when(has_high)
    def _():
        up_edge().start()

    @pl.when(has_low)
    def _():
        down_edge().start()

    @pl.when(has_high)
    def _():
        up_edge().wait_send()
        down_edge().wait_recv()

    @pl.when(has_low)
    def _():
        down_edge().wait_send()
        up_edge().wait_recv()

    mc = lambda r: mc_ref[r : r + 1, :]
    ec = lambda r: ec_ref[r : r + 1, :]

    @pl.loop(0, waves // span)
    def _(i):
        packs = pl.ds(pl.multiple_of(i * 8, 8), 8)
        lows, highs = from_low[packs, :], from_high[packs, :]
        done = []
        for chunk in range(4):
            at = pl.ds(pl.multiple_of(i * span + chunk * 8, 8), 8)
            state = [
                (sre[at, v * 128 : v * 128 + 128], sim[at, v * 128 : v * 128 + 128]) for v in range(3)
            ]
            edge = []
            for part in range(2):
                f = 2 * chunk + part
                tile = jnp.where(spot < 3, roll(lows, -3 * f), roll(highs, 7 - 3 * f))
                for v in range(3):
                    a = state[v][part]
                    mine = jnp.where(spot < 5, roll(a, BLOCK * v + 3), roll(a, BLOCK * v + 7))
                    tile = jnp.where((blk == v) & (spot >= 3) & (spot < 7), mine, tile)
                edge.append(jnp.where((spot < 10) & (blk < 3), tile, 0.0))
            done.append(substeps(state, tuple(edge), kv_ref[0, at, :], kv_ref[1, at, :], mc, ec))
            if chunk % 2 == 0:
                continue
            to = pl.ds(pl.multiple_of(i * span + (chunk - 1) * 8, 16), 16)
            for v in range(3):
                for part in range(2):
                    val = jnp.concatenate([done[chunk - 1][v][part], done[chunk][v][part]], axis=0)
                    high = val.astype(jnp.bfloat16)
                    low = (val - high.astype(jnp.float32)).astype(jnp.bfloat16)
                    if v < 2:
                        sh[part, to, v * 128 : v * 128 + 128] = high
                        sl[part, to, v * 128 : v * 128 + 128] = low
                    else:
                        ss[part, to, 0:128] = high
                        ss[part, to, 128:256] = low

    for t in tables[3:]:
        t.wait()

    def inverse(product, vectors):
        def sums(table, base, half, at):
            out = None
            for part in range(2):
                cols = slice(part * half, part * half + half)
                term = product(table[0, at, cols], table[1, at, cols], part, slice(base, base + half))
                out = term if out is None else out + term
            return out

        piece = 192
        for p in range(0, quarter, piece):
            at = slice(p, p + piece)
            ya, yb = sums(ia, 0, ka, at), sums(ib, ka, kb, at)
            y0, y1 = ya + yb, ya - yb
            o0 = sums(ic, ka + kb, kc, at)
            o1 = sums(ic, ka + kb, kc, slice(quarter + p, quarter + p + piece))
            for n, v in enumerate(vectors):
                lanes = slice(n * 128, n * 128 + 128)
                for s, val in enumerate((y0 + o0, y1 + o1, y0 - o0, y1 - o1)):
                    home[s, v, at, :] = val[:, lanes]

    def send(v):
        for p in (2, 1, 3):
            back(p, v).start()
        own_out(v).start()

    inverse(lambda top, bottom, part, src: single(top, bottom, ss[part, src, :]), (2,))
    send(2)
    inverse(lambda top, bottom, part, src: pair(top, bottom, sh[part, src, :], sl[part, src, :]), (0, 1))
    send(0)
    send(1)
    for v in range(3):
        own_out(v).wait()
        for p in (1, 2, 3):
            go(p, v).wait_send()
            back(p, v).wait()


def local_waves(prognostic, wind_zonal, wind_merid, layer_depth, diffusion):
    col_count, row_count = prognostic.shape[2:]
    total = col_count * 4
    fwd, bwd = wave_tables(total)
    vectors = wave_vectors(total)
    waves = vectors.shape[1]
    vectors = np.ascontiguousarray(np.broadcast_to(vectors[:, :, None], (2, waves, 128)))
    mains, edges = geometry_tables(lax.axis_size("lat"), row_count)
    tables = [jnp.asarray(t) for t in fwd + bwd]
    bf16, f32 = jnp.bfloat16, jnp.float32
    vmem = pl.BlockSpec(memory_space=pltpu.VMEM)
    smem = pl.BlockSpec(memory_space=pltpu.SMEM)
    hbm = pl.BlockSpec(memory_space=pl.ANY)
    dma = pltpu.SemaphoreType.DMA
    return pl.pallas_call(
        wave_kernel,
        out_shape=jax.ShapeDtypeStruct(prognostic.shape, f32),
        in_specs=[hbm, vmem, vmem, smem, smem, vmem, vmem, vmem] + [hbm] * 6,
        out_specs=hbm,
        scratch_shapes=[pltpu.VMEM(t.shape, bf16) for t in tables] + [
            pltpu.VMEM((4, 3, col_count, row_count), f32),
            pltpu.VMEM((4, 3, col_count, row_count), f32),
            pltpu.VMEM((total, 256), bf16),
            pltpu.VMEM((total, 256), bf16),
            pltpu.VMEM((total, 256), bf16),
            pltpu.VMEM((waves, 384), f32),
            pltpu.VMEM((waves, 384), f32),
            pltpu.VMEM((2, waves, 256), bf16),
            pltpu.VMEM((2, waves, 256), bf16),
            pltpu.VMEM((2, waves, 256), bf16),
            pltpu.VMEM((8, 128), f32),
            pltpu.VMEM((2, 8, 128), f32),
            pltpu.VMEM((waves // 4, 128), f32),
            pltpu.VMEM((waves // 4, 128), f32),
            pltpu.VMEM((waves // 4, 128), f32),
            pltpu.VMEM((waves // 4, 128), f32),
            pltpu.VMEM((24, 128), f32),
            pltpu.VMEM((16, 128), f32),
            dma((6,)), dma((2, 3)), dma((4, 3)), dma((4, 3)), dma((4, 3)), dma((4, 3)),
            dma((2,)), dma((2,)), dma((2,)), dma((2,)),
        ],
        compiler_params=pltpu.CompilerParams(
            vmem_limit_bytes=58 * 2**20, collective_id=0, has_side_effects=True
        ),
        name="waves",
    )(prognostic, wind_zonal, wind_merid, layer_depth, diffusion, jnp.asarray(mains), jnp.asarray(edges),
      jnp.asarray(vectors), *tables)


def solution(mesh):
    return jax.shard_map(
        local_waves if mesh.shape["lon"] == 4 else local,
        mesh=mesh,
        in_specs=(P(None, None, "lon", "lat"), P(None, "lat"), P(None, "lat"), P(), P()),
        out_specs=P(None, None, "lon", "lat"),
        check_vma=False,
    )
```

```python
import math

import jax
import jax.numpy as jnp
import ml_dtypes
import numpy as np
from jax import lax
from jax.experimental import pallas as pl
from jax.experimental.pallas import tpu as pltpu
from jax.sharding import PartitionSpec as P

ITERS = 3


time_step = 0.15
highest = lax.Precision.HIGHEST


def with_halo(block, sides, width, periodic):
    for axis, dim in sides:
        count = lax.axis_size(axis)
        forward = [(i, i + 1) for i in range(count - 1)]
        if periodic:
            forward.append((count - 1, 0))
        backward = [(target, source) for source, target in forward]
        low = lax.ppermute(
            lax.slice_in_dim(block, block.shape[dim] - width, None, axis=dim), axis, forward
        )
        high = lax.ppermute(lax.slice_in_dim(block, 0, width, axis=dim), axis, backward)
        block = jnp.concatenate([low, block, high], axis=dim)
    return block


def latitude(row_ids, lat_total):
    return (row_ids.astype(jnp.float32) + 0.5) * (math.pi / lat_total) - 0.5 * math.pi


def damping(row_ids, lat_total, circle_len):
    cos_ratio = jnp.cos(latitude(row_ids, lat_total)) / math.cos(0.25 * math.pi)
    wave_ids = jnp.arange(circle_len // 2 + 1)
    sine_vals = jnp.sin(wave_ids.astype(jnp.float32) * (math.pi / circle_len))
    safe_sines = jnp.where(wave_ids == 0, 1.0, sine_vals)
    return jnp.where(
        wave_ids[None, :] == 0, 1.0, jnp.minimum(1.0, cos_ratio[:, None] / safe_sines[None, :])
    )


def tendency(
    fields_now,
    north_rows,
    south_rows,
    east_cols,
    west_cols,
    row_ids,
    lat_total,
    wind_zonal,
    wind_merid,
    layer_depth,
    diffusion,
):
    latitudes = latitude(row_ids, lat_total)
    cos_centre = jnp.cos(latitudes)
    cos_north = jnp.cos(latitude(row_ids + 1, lat_total))
    cos_south = jnp.cos(latitude(row_ids - 1, lat_total))
    coriolis = jnp.sin(latitudes)
    zonal_diff = (east_cols - west_cols) / (2.0 * cos_centre)
    merid_diff = 0.5 * (north_rows - south_rows)
    advect = wind_zonal[:, None, :] * zonal_diff + wind_merid[:, None, :] * merid_diff
    diverge = zonal_diff[0] + (north_rows[1] * cos_north - south_rows[1] * cos_south) / (
        2.0 * cos_centre
    )
    zonal_tend = -advect[0] + coriolis * fields_now[1] - zonal_diff[2]
    merid_tend = -advect[1] - coriolis * fields_now[0] - merid_diff[2]
    height_tend = -advect[2] - layer_depth[:, None, None] * diverge
    tracer_tend = -advect[3:] + diffusion[:, :, None, None] * (
        north_rows[3:] - 2.0 * fields_now[3:] + south_rows[3:]
    )
    return jnp.concatenate(
        [zonal_tend[None], merid_tend[None], height_tend[None], tracer_tend], axis=0
    )


def split_length(total):
    first = int(math.isqrt(total))
    while total % first != 0:
        first = first - 1
    return (first, total // first)


def trig_table(length):
    counts = jnp.arange(length, dtype=jnp.int32)
    phases = counts[:, None] * counts[None, :] % length
    angles = phases.astype(jnp.float32) * (2.0 * math.pi / length)
    return (jnp.cos(angles), jnp.sin(angles))


def twist_table(outer, inner, total):
    outer_ids = jnp.arange(outer, dtype=jnp.int32)
    inner_ids = jnp.arange(inner, dtype=jnp.int32)
    angles = (outer_ids[:, None] * inner_ids[None, :] % total).astype(jnp.float32) * (
        2.0 * math.pi / total
    )
    return (jnp.cos(angles)[None], jnp.sin(angles)[None])


def forward_real(signal):
    vectors, total = signal.shape
    inner, outer = split_length(total)
    grid = signal.reshape(vectors, outer, inner)
    cos_outer, sin_outer = trig_table(outer)
    first_re = jnp.einsum("mba,bk->mka", grid, cos_outer, precision=highest)
    first_im = -jnp.einsum("mba,bk->mka", grid, sin_outer, precision=highest)
    twist_cos, twist_sin = twist_table(outer, inner, total)
    mid_re = first_re * twist_cos + first_im * twist_sin
    mid_im = first_im * twist_cos - first_re * twist_sin
    cos_inner, sin_inner = trig_table(inner)
    last_re = jnp.einsum("mka,aq->mqk", mid_re, cos_inner, precision=highest) + jnp.einsum(
        "mka,aq->mqk", mid_im, sin_inner, precision=highest
    )
    last_im = jnp.einsum("mka,aq->mqk", mid_im, cos_inner, precision=highest) - jnp.einsum(
        "mka,aq->mqk", mid_re, sin_inner, precision=highest
    )
    return (last_re.reshape(vectors, total), last_im.reshape(vectors, total))


def inverse_real(spec_re, spec_im):
    vectors, total = spec_re.shape
    inner, outer = split_length(total)
    grid_re = spec_re.reshape(vectors, outer, inner)
    grid_im = spec_im.reshape(vectors, outer, inner)
    cos_outer, sin_outer = trig_table(outer)
    first_re = jnp.einsum("mba,bk->mka", grid_re, cos_outer, precision=highest) - jnp.einsum(
        "mba,bk->mka", grid_im, sin_outer, precision=highest
    )
    first_im = jnp.einsum("mba,bk->mka", grid_im, cos_outer, precision=highest) + jnp.einsum(
        "mba,bk->mka", grid_re, sin_outer, precision=highest
    )
    twist_cos, twist_sin = twist_table(outer, inner, total)
    mid_re = first_re * twist_cos - first_im * twist_sin
    mid_im = first_im * twist_cos + first_re * twist_sin
    cos_inner, sin_inner = trig_table(inner)
    last_re = jnp.einsum("mka,aq->mqk", mid_re, cos_inner, precision=highest) - jnp.einsum(
        "mka,aq->mqk", mid_im, sin_inner, precision=highest
    )
    return last_re.reshape(vectors, total)


def local(prognostic, wind_zonal, wind_merid, layer_depth, diffusion):
    field_count, level_count, col_count, row_count = prognostic.shape
    lat_devs = lax.axis_size("lat")
    lon_devs = lax.axis_size("lon")
    lat_total = row_count * lat_devs
    circle_len = col_count * lon_devs
    lat_pos = lax.axis_index("lat")
    lon_pos = lax.axis_index("lon")
    row_ids = lat_pos * row_count + jnp.arange(row_count, dtype=jnp.int32)
    quarter = lat_devs // 4
    is_polar = (lat_pos < quarter) | (lat_pos >= lat_devs - quarter)

    def smooth(sector, start_row):
        vectors, total, slab_rows = sector.shape
        halfway = damping(start_row + jnp.arange(slab_rows, dtype=jnp.int32), lat_total, circle_len)
        mirrored = halfway[:, 1 : circle_len // 2][:, ::-1]
        factors = jnp.concatenate([halfway, mirrored], axis=1)[None]
        rows_last = jnp.transpose(sector, (0, 2, 1)).reshape(vectors * slab_rows, total)
        spec_re, spec_im = forward_real(rows_last)
        spec_re = (spec_re.reshape(vectors, slab_rows, total) * factors).reshape(
            vectors * slab_rows, total
        )
        spec_im = (spec_im.reshape(vectors, slab_rows, total) * factors).reshape(
            vectors * slab_rows, total
        )
        back = inverse_real(spec_re, spec_im) * (1.0 / circle_len)
        return jnp.transpose(back.reshape(vectors, slab_rows, total), (0, 2, 1))

    fields_now = prognostic
    for substep in range(ITERS):
        lat_padded = with_halo(fields_now, (("lat", 3),), 1, False)
        lon_padded = with_halo(fields_now, (("lon", 2),), 1, True)
        tendency_now = tendency(
            fields_now,
            lat_padded[:, :, :, 2:],
            lat_padded[:, :, :, :-2],
            lon_padded[:, :, 2:],
            lon_padded[:, :, :-2],
            row_ids,
            lat_total,
            wind_zonal,
            wind_merid,
            layer_depth,
            diffusion,
        )
        flattened = tendency_now.reshape(field_count * level_count, col_count, row_count)

        def filter_sector(sector):
            slab_rows = sector.shape[2]
            start_row = lat_pos * row_count + lon_pos * slab_rows
            damped = lax.cond(
                is_polar, lambda inner: smooth(inner, start_row), lambda inner: inner, sector
            )
            return lax.all_to_all(damped, "lon", split_axis=1, concat_axis=2, tiled=True)

        filtered = filter_sector(
            lax.all_to_all(flattened, "lon", split_axis=2, concat_axis=1, tiled=True)
        )
        fields_now = fields_now + time_step * filtered.reshape(fields_now.shape)
    return fields_now


HALO = 3
BLOCK = 32
FOLD = 8
MESH = pl.DeviceIdType.MESH


def wave_layout(total):
    q = total // 4
    pad_a = -(-(q // 2 + 1) // 32) * 32
    wave_a = np.full(pad_a, -1)
    wave_a[: q // 2 + 1] = 4 * np.arange(q // 2 + 1)
    wave_b = 4 * np.arange(q // 2) + 2
    wave_c = 2 * np.arange(q) + 1
    return wave_a, wave_b, wave_c


def split_bf16(table):
    table = table.astype(np.float32)
    high = table.astype(ml_dtypes.bfloat16)
    low = (table - high.astype(np.float32)).astype(ml_dtypes.bfloat16)
    return np.stack([high, low])


def wave_tables(total):
    out_fwd, out_inv = [], []
    for waves, width in zip(wave_layout(total), (total // 4, total // 4, total // 2)):
        angle = 2 * np.pi * (waves[:, None] * np.arange(width)[None, :] % total) / total
        real = waves >= 0
        cos = np.where(real[:, None], np.cos(angle), 0.0)
        sin = np.where(real[:, None], np.sin(angle), 0.0)
        weight = np.where((waves == 0) | (2 * waves == total), 1.0, 2.0)[:, None] / total
        out_fwd.append(split_bf16(np.concatenate([cos, -sin], axis=0)))
        out_inv.append(split_bf16(np.concatenate([cos * weight, -sin * weight], axis=0).T))
    return out_fwd, out_inv


def wave_vectors(total):
    waves = np.concatenate(wave_layout(total))
    sigma = np.where(waves >= 0, np.sin(2 * np.pi * waves / total), 0.0)
    sine = np.where(waves > 0, np.sin(np.pi * waves / total), 1.0)
    inverse = np.where(waves == 0, 1e30, 1.0 / sine)
    return np.stack([sigma, inverse]).astype(np.float32)


def geometry(row_ids, lat_total):
    def lat(ids):
        step = np.float32(math.pi / lat_total)
        return ((ids.astype(np.float32) + np.float32(0.5)) * step - np.float32(0.5 * math.pi)).astype(np.float64)

    cos_c = np.cos(lat(row_ids))
    valid = (row_ids >= 0) & (row_ids < lat_total)
    rows = [
        1.0 / cos_c,
        np.sin(lat(row_ids)),
        0.5 * np.cos(lat(row_ids + 1)) / cos_c,
        0.5 * np.cos(lat(row_ids - 1)) / cos_c,
        np.abs(cos_c) / math.cos(0.25 * math.pi),
        np.where(valid, time_step, 0.0),
    ]
    return np.stack(rows + [np.zeros_like(cos_c)] * 2).astype(np.float32)


def geometry_tables(lat_devs, row_count):
    total = lat_devs * row_count
    mains, edges = [], []
    keep = HALO - 1
    offsets = np.concatenate([np.arange(-HALO, keep), np.arange(-keep, HALO) + row_count])
    for pos in range(lat_devs):
        mains.append(geometry(pos * row_count + np.arange(row_count), total))
        short = geometry(pos * row_count + offsets, total)
        wide = np.zeros((8, 128), np.float32)
        for v in range(3):
            wide[:, BLOCK * v : BLOCK * v + len(offsets)] = short
        edges.append(wide)
    return np.stack(mains), np.stack(edges)


def roll(x, shift):
    return pltpu.roll(x, shift % 128, 1)


def substeps(state, edge, sigma, inv_sine, mc, ec):
    lane = lax.broadcasted_iota(jnp.int32, edge[0].shape, 1)
    first, last = lane == 0, lane == 127
    fac = mc(17) * jnp.minimum(1.0, mc(16) * inv_sine)
    efac = ec(12) * jnp.minimum(1.0, ec(11) * inv_sine)
    for step in range(ITERS):
        tends, zons, etend, ezon = [], [], [], []
        for part in range(2):
            a = [state[v][part] for v in range(3)]
            h = edge[part]
            east = [jnp.where(last, roll(h, 120 - BLOCK * v), roll(a[v], 127)) for v in range(3)]
            west = [jnp.where(first, roll(h, 126 - BLOCK * v), roll(a[v], 1)) for v in range(3)]
            t = [mc(v) * east[v] + mc(3 + v) * west[v] + mc(6 + v) * a[v] for v in range(3)]
            t[0] = t[0] + mc(9) * a[1]
            t[1] = t[1] - mc(9) * a[0] - mc(10) * (east[2] - west[2])
            t[2] = t[2] + mc(11) * east[1] + mc(12) * west[1]
            z = [mc(13) * a[v] for v in range(3)]
            z[0] = z[0] + mc(14) * a[2]
            z[2] = z[2] + mc(15) * a[0]
            tends.append(t)
            zons.append(z)
            if step < ITERS - 1:
                etend.append(
                    ec(0) * roll(h, 127) + ec(1) * roll(h, 1) + ec(2) * h
                    + ec(3) * roll(h, -BLOCK) + ec(4) * roll(h, BLOCK)
                    + ec(5) * roll(h, -BLOCK - 1) + ec(6) * roll(h, -BLOCK + 1)
                    + ec(7) * roll(h, BLOCK - 1) + ec(8) * roll(h, BLOCK + 1)
                )
                ezon.append(ec(9) * h + ec(10) * roll(h, 64))
        state = [
            (
                state[v][0] + fac * (tends[0][v] + sigma * zons[1][v]),
                state[v][1] + fac * (tends[1][v] - sigma * zons[0][v]),
            )
            for v in range(3)
        ]
        if step < ITERS - 1:
            edge = (
                edge[0] + efac * (etend[0] + sigma * ezon[1]),
                edge[1] + efac * (etend[1] - sigma * ezon[0]),
            )
    return state


def wave_kernel(
    x_ref, wz_ref, wm_ref, depth_ref, kappa_ref, gm_ref, ge_ref, kv_ref,
    fa_h, fb_h, fc_h, ia_h, ib_h, ic_h, out_ref,
    fa, fb, fc, ia, ib, ic, recv, home, xh, xl, xs, sre, sim, sh, sl, ss,
    wind, wind_in, up, down, from_low, from_high, mc_ref, ec_ref,
    table_sem, own_sem, go_send, go_recv, back_send, back_recv, wind_send, wind_recv, edge_send, edge_recv,
):
    lat, lon = lax.axis_index("lat"), lax.axis_index("lon")
    lat_devs = lax.axis_size("lat")
    quarter = recv.shape[2]
    ka, kb, kc = fa.shape[1] // 2, fb.shape[1] // 2, fc.shape[1] // 2
    waves = ka + kb + kc
    has_low, has_high = lat > 0, lat < lat_devs - 1
    kind, level = lon // 2, lon % 2

    barrier = pltpu.get_barrier_semaphore()
    for p in (1, 2, 3):
        pl.semaphore_signal(barrier, inc=1, device_id=(lat, (lon + p) % 4), device_id_type=MESH)

    @pl.when(has_low)
    def _():
        pl.semaphore_signal(barrier, inc=1, device_id=(lat - 1, lon), device_id_type=MESH)

    @pl.when(has_high)
    def _():
        pl.semaphore_signal(barrier, inc=1, device_id=(lat + 1, lon), device_id_type=MESH)

    pl.semaphore_wait(barrier, 3 + jnp.where(has_low, 1, 0) + jnp.where(has_high, 1, 0))

    def go(p, v):
        to = (lon + p) % 4
        return pltpu.make_async_remote_copy(
            src_ref=x_ref.at[3 * (to // 2) + v, to % 2], dst_ref=recv.at[p, v],
            send_sem=go_send.at[p, v], recv_sem=go_recv.at[p, v],
            device_id=(lat, to), device_id_type=MESH,
        )

    def back(p, v):
        to = (lon + p) % 4
        return pltpu.make_async_remote_copy(
            src_ref=home.at[to, v], dst_ref=out_ref.at[3 * kind + v, level],
            send_sem=back_send.at[p, v], recv_sem=back_recv.at[p, v],
            device_id=(lat, to), device_id_type=MESH,
        )

    def own_in(v):
        return pltpu.make_async_copy(x_ref.at[3 * kind + v, level], recv.at[0, v], own_sem.at[0, v])

    def own_out(v):
        return pltpu.make_async_copy(home.at[lon, v], out_ref.at[3 * kind + v, level], own_sem.at[1, v])

    def beside(src, dst, side, send_sem, recv_sem):
        return pltpu.make_async_remote_copy(
            src_ref=src, dst_ref=dst, send_sem=send_sem.at[side], recv_sem=recv_sem.at[side],
            device_id=((lat + (1 if side == 0 else lat_devs - 1)) % lat_devs, lon), device_id_type=MESH,
        )

    for v in range(3):
        for p in (2, 1, 3):
            go(p, v).start()
        own_in(v).start()
    tables = [
        pltpu.make_async_copy(src, dst, table_sem.at[i])
        for i, (src, dst) in enumerate(
            ((fa_h, fa), (fb_h, fb), (fc_h, fc), (ia_h, ia), (ib_h, ib), (ic_h, ic))
        )
    ]
    for t in tables:
        t.start()

    wind[0:2, :] = wz_ref[...]
    wind[2:4, :] = wm_ref[...]
    wind[4:8, :] = jnp.zeros((4, 128), jnp.float32)
    up_wind = lambda: beside(wind, wind_in.at[0], 0, wind_send, wind_recv)
    down_wind = lambda: beside(wind, wind_in.at[1], 1, wind_send, wind_recv)
    up_edge = lambda: beside(up, from_low, 0, edge_send, edge_recv)
    down_edge = lambda: beside(down, from_high, 1, edge_send, edge_recv)

    @pl.when(has_high)
    def _():
        up_wind().start()

    @pl.when(has_low)
    def _():
        down_wind().start()

    @pl.when(jnp.logical_not(has_low))
    def _():
        wind_in[0] = jnp.zeros((8, 128), jnp.float32)
        from_low[...] = jnp.zeros(from_low.shape, jnp.float32)

    @pl.when(jnp.logical_not(has_high))
    def _():
        wind_in[1] = jnp.zeros((8, 128), jnp.float32)
        from_high[...] = jnp.zeros(from_high.shape, jnp.float32)

    @pl.when(has_high)
    def _():
        up_wind().wait_send()
        down_wind().wait_recv()

    @pl.when(has_low)
    def _():
        down_wind().wait_send()
        up_wind().wait_recv()

    lane8 = lax.broadcasted_iota(jnp.int32, (8, 128), 1)
    spot8, block8 = lane8 % BLOCK, lane8 // BLOCK
    dyn = jnp.where(lon < 2, 1.0, 0.0).astype(jnp.float32)
    depth = depth_ref[level] * dyn
    kappa = [kappa_ref[v, level] * (1.0 - dyn) for v in range(3)]
    row = lambda ref, r: ref[lat, r : r + 1, :]
    wz, wm = wind[pl.ds(level, 1), :], wind[pl.ds(2 + level, 1), :]
    one = jnp.ones((1, 128), jnp.float32)
    inv, rot, cn, cs = (row(gm_ref, r) for r in range(4))
    coefs = (
        [kappa[v] - 0.5 * wm for v in range(3)] + [kappa[v] + 0.5 * wm for v in range(3)]
        + [-2.0 * kappa[v] * one for v in range(3)]
        + [dyn * rot, 0.5 * dyn * one, -depth * cn, depth * cs, wz * inv, dyn * inv, depth * inv, row(gm_ref, 4), row(gm_ref, 5)]
    )
    for r, c in enumerate(coefs):
        mc_ref[r : r + 1, :] = c

    below = jnp.where(lane8 >= 128 - HALO, wind_in[0], wind[...])
    above = jnp.where(lane8 < HALO, wind_in[1], wind[...])
    ewind = jnp.zeros((8, 128), jnp.float32)
    for v in range(3):
        val = jnp.where(spot8 < 5, roll(below, BLOCK * v + 3), roll(above, BLOCK * v + 7))
        ewind = jnp.where(block8 == v, val, ewind)
    used = (spot8 < 10) & (block8 < 3)
    ewind = jnp.where(used, ewind, 0.0)
    ec_ref[0:8, :] = ewind
    ez, em = ec_ref[pl.ds(level, 1), :], ec_ref[pl.ds(2 + level, 1), :]
    block = block8[0:1]
    only = lambda v, val: jnp.where(block == v, val, 0.0)
    ekap = only(0, kappa[0] * one) + only(1, kappa[1] * one) + only(2, kappa[2] * one)
    inv, rot, cn, cs = (row(ge_ref, r) for r in range(4))
    coefs = [
        ekap - 0.5 * em, ekap + 0.5 * em, -2.0 * ekap,
        only(0, dyn * rot), only(1, -dyn * rot), only(1, -0.5 * dyn * one), only(1, 0.5 * dyn * one),
        only(2, -depth * cn), only(2, depth * cs), ez * inv, only(0, dyn * inv) + only(2, depth * inv),
        row(ge_ref, 4), row(ge_ref, 5),
    ]
    for r, c in enumerate(coefs):
        ec_ref[r : r + 1, :] = c

    rows = 16
    slots = [(lon - s + 4) % 4 for s in range(4)]

    def split_in(v):
        @pl.loop(0, quarter // rows)
        def _(i):
            at = pl.ds(pl.multiple_of(i * rows, rows), rows)
            x = [recv[slots[s], v, at, :] for s in range(4)]
            y0, y1 = x[0] + x[2], x[1] + x[3]
            for part, val in enumerate((y0 + y1, y0 - y1, x[0] - x[2], x[1] - x[3])):
                high = val.astype(jnp.bfloat16)
                low = (val - high.astype(jnp.float32)).astype(jnp.bfloat16)
                to = pl.ds(pl.multiple_of(part * quarter + i * rows, rows), rows)
                if v < 2:
                    xh[to, v * 128 : v * 128 + 128] = high
                    xl[to, v * 128 : v * 128 + 128] = low
                else:
                    xs[to, 0:128] = high
                    xs[to, 128:256] = low

    dot = lambda p, q: jnp.dot(p, q, preferred_element_type=jnp.float32)

    def pair(top, bottom, high, low):
        return dot(top, high) + dot(bottom, high) + dot(top, low)

    def single(top, bottom, both):
        full = dot(top, both)
        return full[:, :128] + full[:, 128:] + dot(bottom, both[:, :128])

    def forward(lanes, product):
        for table, half, base, start, size in (
            (fa, ka, 0, 0, quarter), (fb, kb, ka, quarter, quarter), (fc, kc, ka + kb, 2 * quarter, 2 * quarter)
        ):
            src = slice(start, start + size)
            full = product(table[0], table[1], src)
            sre[base : base + half, lanes] = full[:half]
            sim[base : base + half, lanes] = full[half:]

    def arrived(v):
        for p in (1, 2, 3):
            go(p, v).wait_recv()
        own_in(v).wait()

    arrived(0)
    split_in(0)
    arrived(1)
    split_in(1)
    for t in tables[:3]:
        t.wait()
    forward(slice(0, 256), lambda top, bottom, src: pair(top, bottom, xh[src, :], xl[src, :]))
    arrived(2)
    split_in(2)
    forward(slice(256, 384), lambda top, bottom, src: single(top, bottom, xs[src, :]))

    lane = lax.broadcasted_iota(jnp.int32, (8, 128), 1)
    spot, blk = lane % BLOCK, lane // BLOCK
    span = 4 * FOLD

    @pl.loop(0, waves // span)
    def _(i):
        ups = jnp.zeros((8, 128), jnp.float32)
        downs = ups
        for f in range(FOLD):
            at = pl.ds(pl.multiple_of(i * span + (f // 2) * 8, 8), 8)
            src = (sre, sim)[f % 2]
            here = (spot >= 3 * f) & (spot < 3 * f + 3)
            for v in range(3):
                a = src[at, v * 128 : v * 128 + 128]
                mask = here & (blk == v)
                ups = jnp.where(mask, roll(a, BLOCK * v + 3 * f + 3), ups)
                downs = jnp.where(mask, roll(a, BLOCK * v + 3 * f), downs)
        to = pl.ds(pl.multiple_of(i * 8, 8), 8)
        up[to, :] = ups
        down[to, :] = downs

    @pl.when(has_high)
    def _():
        up_edge().start()

    @pl.when(has_low)
    def _():
        down_edge().start()

    @pl.when(has_high)
    def _():
        up_edge().wait_send()
        down_edge().wait_recv()

    @pl.when(has_low)
    def _():
        down_edge().wait_send()
        up_edge().wait_recv()

    mc = lambda r: mc_ref[r : r + 1, :]
    ec = lambda r: ec_ref[r : r + 1, :]

    @pl.loop(0, waves // span)
    def _(i):
        packs = pl.ds(pl.multiple_of(i * 8, 8), 8)
        lows, highs = from_low[packs, :], from_high[packs, :]
        done = []
        for chunk in range(4):
            at = pl.ds(pl.multiple_of(i * span + chunk * 8, 8), 8)
            state = [
                (sre[at, v * 128 : v * 128 + 128], sim[at, v * 128 : v * 128 + 128]) for v in range(3)
            ]
            edge = []
            for part in range(2):
                f = 2 * chunk + part
                tile = jnp.where(spot < 3, roll(lows, -3 * f), roll(highs, 7 - 3 * f))
                for v in range(3):
                    a = state[v][part]
                    mine = jnp.where(spot < 5, roll(a, BLOCK * v + 3), roll(a, BLOCK * v + 7))
                    tile = jnp.where((blk == v) & (spot >= 3) & (spot < 7), mine, tile)
                edge.append(jnp.where((spot < 10) & (blk < 3), tile, 0.0))
            done.append(substeps(state, tuple(edge), kv_ref[0, at, :], kv_ref[1, at, :], mc, ec))
            if chunk % 2 == 0:
                continue
            to = pl.ds(pl.multiple_of(i * span + (chunk - 1) * 8, 16), 16)
            for v in range(3):
                for part in range(2):
                    val = jnp.concatenate([done[chunk - 1][v][part], done[chunk][v][part]], axis=0)
                    high = val.astype(jnp.bfloat16)
                    low = (val - high.astype(jnp.float32)).astype(jnp.bfloat16)
                    if v < 2:
                        sh[part, to, v * 128 : v * 128 + 128] = high
                        sl[part, to, v * 128 : v * 128 + 128] = low
                    else:
                        ss[part, to, 0:128] = high
                        ss[part, to, 128:256] = low

    for t in tables[3:]:
        t.wait()

    def inverse(product, vectors):
        def sums(table, base, half):
            out = None
            for part in range(2):
                cols = slice(part * half, part * half + half)
                term = product(table[0, :, cols], table[1, :, cols], part, slice(base, base + half))
                out = term if out is None else out + term
            return out

        ya, yb = sums(ia, 0, ka), sums(ib, ka, kb)
        y0, y1 = ya + yb, ya - yb
        odd = sums(ic, ka + kb, kc)
        o0, o1 = odd[:quarter], odd[quarter:]
        for n, v in enumerate(vectors):
            lanes = slice(n * 128, n * 128 + 128)
            for s, val in enumerate((y0 + o0, y1 + o1, y0 - o0, y1 - o1)):
                home[s, v] = val[:, lanes]

    def send(v):
        for p in (2, 1, 3):
            back(p, v).start()
        own_out(v).start()

    inverse(lambda top, bottom, part, src: single(top, bottom, ss[part, src, :]), (2,))
    send(2)
    inverse(lambda top, bottom, part, src: pair(top, bottom, sh[part, src, :], sl[part, src, :]), (0, 1))
    send(0)
    send(1)
    for v in range(3):
        own_out(v).wait()
        for p in (1, 2, 3):
            go(p, v).wait_send()
            back(p, v).wait()


def local_waves(prognostic, wind_zonal, wind_merid, layer_depth, diffusion):
    col_count, row_count = prognostic.shape[2:]
    total = col_count * 4
    fwd, bwd = wave_tables(total)
    vectors = wave_vectors(total)
    waves = vectors.shape[1]
    vectors = np.ascontiguousarray(np.broadcast_to(vectors[:, :, None], (2, waves, 128)))
    mains, edges = geometry_tables(lax.axis_size("lat"), row_count)
    tables = [jnp.asarray(t) for t in fwd + bwd]
    bf16, f32 = jnp.bfloat16, jnp.float32
    vmem = pl.BlockSpec(memory_space=pltpu.VMEM)
    smem = pl.BlockSpec(memory_space=pltpu.SMEM)
    hbm = pl.BlockSpec(memory_space=pl.ANY)
    dma = pltpu.SemaphoreType.DMA
    return pl.pallas_call(
        wave_kernel,
        out_shape=jax.ShapeDtypeStruct(prognostic.shape, f32),
        in_specs=[hbm, vmem, vmem, smem, smem, vmem, vmem, vmem] + [hbm] * 6,
        out_specs=hbm,
        scratch_shapes=[pltpu.VMEM(t.shape, bf16) for t in tables] + [
            pltpu.VMEM((4, 3, col_count, row_count), f32),
            pltpu.VMEM((4, 3, col_count, row_count), f32),
            pltpu.VMEM((total, 256), bf16),
            pltpu.VMEM((total, 256), bf16),
            pltpu.VMEM((total, 256), bf16),
            pltpu.VMEM((waves, 384), f32),
            pltpu.VMEM((waves, 384), f32),
            pltpu.VMEM((2, waves, 256), bf16),
            pltpu.VMEM((2, waves, 256), bf16),
            pltpu.VMEM((2, waves, 256), bf16),
            pltpu.VMEM((8, 128), f32),
            pltpu.VMEM((2, 8, 128), f32),
            pltpu.VMEM((waves // 4, 128), f32),
            pltpu.VMEM((waves // 4, 128), f32),
            pltpu.VMEM((waves // 4, 128), f32),
            pltpu.VMEM((waves // 4, 128), f32),
            pltpu.VMEM((24, 128), f32),
            pltpu.VMEM((16, 128), f32),
            dma((6,)), dma((2, 3)), dma((4, 3)), dma((4, 3)), dma((4, 3)), dma((4, 3)),
            dma((2,)), dma((2,)), dma((2,)), dma((2,)),
        ],
        compiler_params=pltpu.CompilerParams(
            vmem_limit_bytes=58 * 2**20, collective_id=0, has_side_effects=True
        ),
        name="waves",
    )(prognostic, wind_zonal, wind_merid, layer_depth, diffusion, jnp.asarray(mains), jnp.asarray(edges),
      jnp.asarray(vectors), *tables)


def solution(mesh):
    return jax.shard_map(
        local_waves if mesh.shape["lon"] == 4 else local,
        mesh=mesh,
        in_specs=(P(None, None, "lon", "lat"), P(None, "lat"), P(None, "lat"), P(), P()),
        out_specs=P(None, None, "lon", "lat"),
        check_vma=False,
    )
```
